32 devices in a mesh: expert: 8 (over z, core), dp: 4 (over y, x).
Axes of the slice: x: 2, y: 2, z: 4, core: 2. Of those that a mesh axis runs over, the one named last changes fastest.
Arguments:
- tokens: bfloat16 [4096, 3584], P(('expert', 'dp')), may hold values from -6 to 6
- expert_ids: int32 [4096, 8], P(('expert', 'dp')), may hold values from 0 to 63, all different within a row
- gate_probs: float32 [4096, 8], P(('expert', 'dp')), may hold values from 0.02 to 0.5
- out_grad: bfloat16 [4096, 3584], P(('expert', 'dp')), may hold values from -6 to 6
- w_gate: bfloat16 [8, 1024, 3584], P('expert', 'dp'), may hold values from -0.09375 to 0.09375
- w_up: bfloat16 [8, 1024, 3584], P('expert', 'dp'), may hold values from -0.09375 to 0.09375
- w_down: bfloat16 [8, 1024, 3584], P('expert', 'dp'), may hold values from -0.1875 to 0.1875
Outputs:
- grad_gate: bfloat16 [8, 1024, 3584], P('expert', 'dp')
- grad_up: bfloat16 [8, 1024, 3584], P('expert', 'dp')
- grad_down: bfloat16 [8, 1024, 3584], P('expert', 'dp')
The draws below stay inside these ranges and needn't reach their ends.
All inputs are finite; a program needn't handle non-finite values.
Results may differ from the reference program's by a relative error of at most 0.0058.
Values may be sent and summed in bfloat16 or wider, within the bound.
No kernel may reach another device: no remote copies, remote signals or barrier semaphores. Data moves between devices by JAX's collectives and lax.ppermute only.
A program may use at most 64 MiB of HBM per device.

```python
import math
import jax
import jax.numpy as jnp
from jax import lax

D = 3584
FF = 1024
TOPK = 8
CAP = 2
TOK_DEV = 128
EXPERTS = 8
TOTAL_EXP = 64
TOKENS = 4096
N_EXPERT = 8
N_DP = 4


def steps_of(rng, dims, shards, least, high):
    gain, own = 1.0, jax.random.fold_in(rng, 6)
    for axis_at, blocks in shards:
        heights = jnp.exp(jax.random.uniform(jax.random.fold_in(own, axis_at), (blocks,), jnp.float32, least / len(shards), high / len(shards)))
        gain = gain * jnp.repeat(heights, dims[axis_at] // blocks).reshape([-1 if axis == axis_at else 1 for axis in range(len(dims))])
    return gain


def picks_of(rng, rows, count, top, lift):
    order = jax.random.permutation(jax.random.fold_in(rng, 1), count)
    boost = order
    for power in range(3):
        boost = boost * boost // count
    boost = boost * lift // count
    tickets = jax.random.randint(jax.random.fold_in(rng, 2), (rows, count), 0, 4096) + boost
    holders = jax.random.permutation(jax.random.fold_in(rng, 3), rows)[jnp.arange(count) % rows]
    tickets = jnp.where(jnp.arange(rows)[:, None] == holders[None, :], 1 << 14, tickets)
    priority = tickets * count + jnp.arange(count)
    return lax.top_k(priority.astype(jnp.int32), top)[1].astype(jnp.int32)


def scatter_about(stream_key, extent, spread, most, cuts=(), kind=jnp.bfloat16):
    gain = steps_of(stream_key, extent, cuts, -0.22, 0.18) if cuts else 1.0
    result = jax.random.normal(stream_key, extent, jnp.float32) * spread * gain
    return jnp.minimum(jnp.maximum(result, -most), most).astype(kind)


def setup_inputs(seed: int = 0) -> dict:
    keys = jax.random.split(jax.random.key(seed), 8)
    return {
        "tokens": scatter_about(keys[0], (TOKENS, D), 1.0, 6.0, ((0, 32),)),
        "expert_ids": picks_of(keys[1], TOKENS, TOTAL_EXP, TOPK, 2048),
        "gate_probs": jnp.clip(jnp.exp(math.log(0.5) - 3.218876 * jax.random.uniform(keys[2], (TOKENS, TOPK), jnp.float32) ** steps_of(keys[2], (TOKENS, TOPK), ((0, 32),), -0.2, 0.2)), 0.02, 0.5),
        "out_grad": scatter_about(keys[3], (TOKENS, D), 1.0, 6.0, ((0, 32),)),
        "w_gate": scatter_about(keys[4], (EXPERTS, FF, D), D ** -0.5, 0.09375, ((0, 8), (1, 4))),
        "w_up": scatter_about(keys[5], (EXPERTS, FF, D), D ** -0.5, 0.09375, ((0, 8), (1, 4))),
        "w_down": scatter_about(keys[6], (EXPERTS, FF, D), FF ** -0.5, 0.1875, ((0, 8), (1, 4))),
    }


def expert_grads(rows_x, rows_dy, weight_gate, weight_up, weight_down):
    gate_pre = jnp.dot(rows_x, weight_gate.T, preferred_element_type=jnp.float32)
    up_pre = jnp.dot(rows_x, weight_up.T, preferred_element_type=jnp.float32)
    back_grad = jnp.dot(rows_dy, weight_down.T, preferred_element_type=jnp.float32)
    sig_gate = jax.nn.sigmoid(gate_pre)
    act_gate = gate_pre * sig_gate
    hidden = (act_gate * up_pre).astype(jnp.bfloat16)
    d_gate = (back_grad * up_pre * sig_gate * (1.0 + gate_pre * (1.0 - sig_gate))).astype(jnp.bfloat16)
    d_up = (back_grad * act_gate).astype(jnp.bfloat16)
    grad_gate = jnp.dot(d_gate.T, rows_x, preferred_element_type=jnp.float32)
    grad_up = jnp.dot(d_up.T, rows_x, preferred_element_type=jnp.float32)
    grad_down = jnp.dot(hidden.T, rows_dy, preferred_element_type=jnp.float32)
    return (grad_gate.astype(jnp.bfloat16), grad_up.astype(jnp.bfloat16), grad_down.astype(jnp.bfloat16))


def reference(tokens, expert_ids, gate_probs, out_grad, w_gate, w_up, w_down):
    blocks = N_EXPERT * N_DP
    per_block = TOK_DEV * TOPK
    ids_block = expert_ids.reshape(blocks, per_block).astype(jnp.int32)
    probs_block = gate_probs.reshape(blocks, per_block)
    expert_range = jnp.arange(EXPERTS, dtype=jnp.int32)
    onehot = (ids_block[:, :, None] == expert_range[None, None, :]).astype(jnp.int32)
    before = jnp.cumsum(onehot, axis=1) - onehot
    slot_rank = jnp.sum(before * onehot, axis=2).astype(jnp.int32)
    kept = (ids_block < EXPERTS) & (slot_rank < CAP)
    block_index = jnp.broadcast_to(jnp.arange(blocks, dtype=jnp.int32)[:, None], (blocks, per_block))
    token_index = (block_index * TOK_DEV + jnp.arange(per_block, dtype=jnp.int32)[None, :] // TOPK).astype(jnp.int32)
    dest_expert = jnp.where(kept, ids_block, EXPERTS).astype(jnp.int32)
    dest_slot = jnp.where(kept, slot_rank, 0).astype(jnp.int32)
    table = jnp.full((EXPERTS, blocks, CAP), TOKENS, jnp.int32)
    table = table.at[dest_expert, block_index, dest_slot].set(token_index, mode="drop")
    prob_table = jnp.zeros((EXPERTS, blocks, CAP), jnp.float32)
    prob_table = prob_table.at[dest_expert, block_index, dest_slot].set(probs_block, mode="drop")

    def one_expert(expert):
        row_ids = table[expert].reshape(-1)
        row_probs = prob_table[expert].reshape(-1)
        rows_x = jnp.take(tokens, row_ids, axis=0, mode="fill", fill_value=0)
        grads_in = jnp.take(out_grad, row_ids, axis=0, mode="fill", fill_value=0)
        rows_dy = (grads_in.astype(jnp.float32) * row_probs[:, None]).astype(jnp.bfloat16)
        return expert_grads(rows_x, rows_dy, w_gate[expert], w_up[expert], w_down[expert])

    grad_gate, grad_up, grad_down = lax.map(one_expert, jnp.arange(EXPERTS, dtype=jnp.int32))
    return (grad_gate, grad_up, grad_down)
```

```python
import functools

import jax
import jax.numpy as jnp
from jax import lax
from jax.experimental import pallas as pl
from jax.experimental.pallas import tpu as pltpu
from jax.sharding import PartitionSpec as P

CAP = 2


def pick_kernel(experts, order_ref, ids_ref, probs_ref, tokens_hbm, grad_hbm, out_ref, tok_buf, grad_buf, sems):
    pieces = sems.shape[1]
    width = tok_buf.shape[1] // pieces
    copies = []
    for part in range(pieces):
        cols = pl.ds(part * width, width)
        copies.append(
            (
                pltpu.make_async_copy(tokens_hbm.at[:, cols], tok_buf.at[:, cols], sems.at[0, part]),
                pltpu.make_async_copy(grad_hbm.at[:, cols], grad_buf.at[:, cols], sems.at[1, part]),
            )
        )
    for copy_x, copy_dy in copies:
        copy_x.start()
        copy_dy.start()
    top, count = ids_ref.shape
    order = order_ref[...]
    named = jnp.zeros((experts, count), jnp.float32)
    prob = jnp.zeros((experts, count), jnp.float32)
    for k in range(top):
        hit = ids_ref[k : k + 1, :] == order
        named = jnp.where(hit, 1.0, named)
        prob = jnp.where(hit, probs_ref[k : k + 1, :], prob)
    earlier = (
        lax.broadcasted_iota(jnp.int32, (count, count), 0)
        < lax.broadcasted_iota(jnp.int32, (count, count), 1)
    ).astype(jnp.bfloat16)
    rank = jnp.dot(named.astype(jnp.bfloat16), earlier, preferred_element_type=jnp.float32)
    pickers = []
    for slot in range(CAP):
        pickers.append(jnp.where((named > 0.5) & (rank == float(slot)), 1.0, 0.0))
    weights = [jnp.sum(picker * prob, axis=1, keepdims=True) for picker in pickers]
    picker = jnp.stack(pickers, axis=1).reshape(experts * CAP, count).astype(jnp.bfloat16)
    weight = jnp.stack(weights, axis=1).reshape(experts * CAP, 1)
    for part in range(pieces):
        cols = pl.ds(part * width, width)
        copy_x, copy_dy = copies[part]
        copy_x.wait()
        rows_x = jnp.dot(picker, tok_buf[:, cols], preferred_element_type=jnp.float32)
        out_ref[:, 0:CAP, cols] = rows_x.reshape(experts, CAP, width).astype(jnp.bfloat16)
        copy_dy.wait()
        rows_dy = jnp.dot(picker, grad_buf[:, cols], preferred_element_type=jnp.float32) * weight
        out_ref[:, CAP : 2 * CAP, cols] = rows_dy.reshape(experts, CAP, width).astype(jnp.bfloat16)


def pick_rows(order, ids, probs, tokens, out_grad):
    experts = order.shape[0]
    count, channels = tokens.shape
    pieces = 4
    vmem = pl.BlockSpec(memory_space=pltpu.VMEM)
    hbm = pl.BlockSpec(memory_space=pltpu.HBM)
    return pl.pallas_call(
        functools.partial(pick_kernel, experts),
        out_shape=jax.ShapeDtypeStruct((experts, 2 * CAP, channels), jnp.bfloat16),
        in_specs=[vmem, vmem, vmem, hbm, hbm],
        out_specs=vmem,
        scratch_shapes=[
            pltpu.VMEM((count, channels), jnp.bfloat16),
            pltpu.VMEM((count, channels), jnp.bfloat16),
            pltpu.SemaphoreType.DMA((2, pieces)),
        ],
        compiler_params=pltpu.CompilerParams(vmem_limit_bytes=16 * 1024 * 1024),
    )(order, ids, probs, tokens, out_grad)


def grads_kernel(rows_ref, gate_ref, up_ref, down_ref, out_gate, out_up, out_down, buf, sems):
    rows = rows_ref[...]
    count, channels = rows.shape
    contract = (((1,), (1,)), ((), ()))
    gate_pre = lax.dot_general(rows, gate_ref[...], contract, preferred_element_type=jnp.float32)
    up_pre = lax.dot_general(rows, up_ref[...], contract, preferred_element_type=jnp.float32)
    back_grad = lax.dot_general(rows, down_ref[...], contract, preferred_element_type=jnp.float32)
    back_grad = pltpu.roll(back_grad, count - CAP, 0)
    is_x = lax.broadcasted_iota(jnp.int32, (count, 1), 0) % (2 * CAP) < CAP
    sig_gate = jax.nn.sigmoid(gate_pre)
    act_gate = gate_pre * sig_gate
    hidden = jnp.where(is_x, act_gate * up_pre, 0.0)
    d_gate = jnp.where(is_x, back_grad * up_pre * sig_gate * (1.0 + gate_pre * (1.0 - sig_gate)), 0.0)
    d_up = jnp.where(is_x, back_grad * act_gate, 0.0)
    hidden = pltpu.roll(hidden, CAP, 0)
    pieces = sems.shape[1]
    width = channels // pieces
    copies = []
    for number, (factor, out) in enumerate(((hidden, out_down), (d_up, out_up), (d_gate, out_gate))):
        turned = factor.T.astype(jnp.bfloat16)
        for part in range(pieces):
            cols = pl.ds(part * width, width)
            term = jnp.dot(turned, rows_ref[:, cols], preferred_element_type=jnp.float32)
            buf[number, :, cols] = term.astype(jnp.bfloat16)
            copy = pltpu.make_async_copy(buf.at[number, :, cols], out.at[:, cols], sems.at[number, part])
            copy.start()
            copies.append(copy)
    for copy in copies:
        copy.wait()


def weight_grads(rows, w_gate, w_up, w_down):
    units, channels = w_gate.shape
    pieces = 4
    vmem = pl.BlockSpec(memory_space=pltpu.VMEM)
    hbm = pl.BlockSpec(memory_space=pltpu.HBM)
    shape = jax.ShapeDtypeStruct((units, channels), jnp.bfloat16)
    return pl.pallas_call(
        grads_kernel,
        out_shape=(shape, shape, shape),
        in_specs=[vmem] * 4,
        out_specs=(hbm, hbm, hbm),
        scratch_shapes=[
            pltpu.VMEM((3, units, channels), jnp.bfloat16),
            pltpu.SemaphoreType.DMA((3, pieces)),
        ],
        compiler_params=pltpu.CompilerParams(vmem_limit_bytes=20 * 1024 * 1024),
    )(rows, w_gate, w_up, w_down)


def local(tokens, expert_ids, gate_probs, out_grad, w_gate, w_up, w_down):
    n_expert = lax.axis_size("expert")
    experts_all = w_gate.shape[0] * n_expert
    channels = tokens.shape[1]
    order = jnp.arange(experts_all, dtype=jnp.int32)[:, None]
    sent = pick_rows(order, expert_ids.T, gate_probs.T, tokens, out_grad)
    recv = lax.all_to_all(sent, "expert", split_axis=0, concat_axis=0, tiled=True)
    rows = lax.all_gather(recv.reshape(-1, channels), "dp", axis=0, tiled=True)
    grads = weight_grads(rows, w_gate[0], w_up[0], w_down[0])
    return tuple(grad[None] for grad in grads)


def solution(mesh):
    in_specs = (
        P(("expert", "dp"), None),
        P(("expert", "dp"), None),
        P(("expert", "dp"), None),
        P(("expert", "dp"), None),
        P("expert", "dp", None),
        P("expert", "dp", None),
        P("expert", "dp", None),
    )
    out_specs = (P("expert", "dp", None), P("expert", "dp", None), P("expert", "dp", None))
    return jax.shard_map(local, mesh=mesh, in_specs=in_specs, out_specs=out_specs, check_vma=False)
```

```python
import functools

import jax
import jax.numpy as jnp
from jax import lax
from jax.experimental import pallas as pl
from jax.experimental.pallas import tpu as pltpu
from jax.sharding import PartitionSpec as P

CAP = 2
ROWS = 2 * CAP
MIB = 1024 * 1024

VMEM = pl.BlockSpec(memory_space=pltpu.VMEM)
HBM = pl.BlockSpec(memory_space=pltpu.HBM)


def in_hbm(*arrays):
    return [pltpu.with_memory_space_constraint(array, pltpu.HBM) for array in arrays]


def pick_kernel(ids_hbm, probs_hbm, tokens_hbm, grad_hbm, own_ref, other_ref, ids_buf, probs_buf, buf, sems):
    copy_ids = pltpu.make_async_copy(ids_hbm, ids_buf, sems.at[0])
    copy_probs = pltpu.make_async_copy(probs_hbm, probs_buf, sems.at[1])
    copy_ids.start()
    copy_probs.start()
    pieces = (sems.shape[0] - 2) // 2
    top, count = ids_buf.shape
    width = buf.shape[1] // pieces
    copies = []
    for part in range(pieces):
        cols = pl.ds(part * width, width)
        for number, source in enumerate((tokens_hbm, grad_hbm)):
            copy = pltpu.make_async_copy(
                source.at[:, cols], buf.at[pl.ds(number * count, count), cols], sems.at[2 + 2 * part + number]
            )
            copy.start()
            copies.append(copy)
    half = own_ref.shape[0]
    total = 2 * half
    row = lax.broadcasted_iota(jnp.int32, (total, 1), 0)
    block = row // ROWS
    places = total // ROWS // 2
    relative = 2 * (block % places) + block // places
    expert = lax.axis_index("expert") ^ relative
    slot = (row % CAP).astype(jnp.float32)
    is_x = row % ROWS < CAP
    earlier = (
        lax.broadcasted_iota(jnp.int32, (count, count), 0)
        < lax.broadcasted_iota(jnp.int32, (count, count), 1)
    ).astype(jnp.bfloat16)
    copy_ids.wait()
    copy_probs.wait()
    named = jnp.zeros((total, count), jnp.float32)
    prob = jnp.zeros((total, count), jnp.float32)
    for k in range(top):
        hit = ids_buf[k : k + 1, :] == expert
        named = jnp.where(hit, 1.0, named)
        prob = jnp.where(hit, probs_buf[k : k + 1, :], prob)
    rank = jnp.dot(named.astype(jnp.bfloat16), earlier, preferred_element_type=jnp.float32)
    pick = jnp.where((named > 0.5) & (rank == slot), 1.0, 0.0)
    scale = jnp.where(is_x, 1.0, jnp.sum(pick * prob, axis=1, keepdims=True))
    picker = jnp.concatenate([jnp.where(is_x, pick, 0.0), jnp.where(is_x, 0.0, pick)], axis=1).astype(jnp.bfloat16)
    for part in range(pieces):
        cols = pl.ds(part * width, width)
        copies[2 * part].wait()
        copies[2 * part + 1].wait()
        rows = jnp.dot(picker, buf[:, cols], preferred_element_type=jnp.float32) * scale
        rows = rows.astype(jnp.bfloat16)
        own_ref[:, cols] = rows[:half]
        other_ref[:, cols] = rows[half:]


def pick_rows(experts, ids, probs, tokens, out_grad):
    top = ids.shape[0]
    count, channels = tokens.shape
    pieces = 4
    shape = pltpu.VMEM((experts * ROWS // 2, channels), jnp.bfloat16)
    return pl.pallas_call(
        pick_kernel,
        out_shape=(shape, shape),
        in_specs=[HBM] * 4,
        out_specs=(VMEM, VMEM),
        scratch_shapes=[
            pltpu.VMEM((top, count), jnp.int32),
            pltpu.VMEM((top, count), jnp.float32),
            pltpu.VMEM((2 * count, channels), jnp.bfloat16),
            pltpu.SemaphoreType.DMA((2 + 2 * pieces,)),
        ],
        compiler_params=pltpu.CompilerParams(vmem_limit_bytes=16 * MIB),
    )(*in_hbm(ids, probs, tokens, out_grad))


def load_kernel(*refs):
    gate_hbm, up_hbm, down_hbm, gate_ref, up_ref, down_ref, sems = refs[-7:]
    copies = []
    for number, (source, target) in enumerate(((gate_hbm, gate_ref), (up_hbm, up_ref), (down_hbm, down_ref))):
        half = source.shape[0] // 2
        for part in range(2):
            rows = pl.ds(part * half, half)
            copy = pltpu.make_async_copy(source.at[rows], target.at[rows], sems.at[number, part])
            copy.start()
            copies.append(copy)
    for copy in copies:
        copy.wait()


def load_weights(after, w_gate, w_up, w_down):
    shape = pltpu.VMEM(w_gate.shape, w_gate.dtype)
    size = w_gate.size * 2
    return pl.pallas_call(
        load_kernel,
        out_shape=(shape, shape, shape),
        in_specs=[pl.BlockSpec(memory_space=pl.ANY)] * len(after) + [HBM] * 3,
        out_specs=(VMEM, VMEM, VMEM),
        scratch_shapes=[pltpu.SemaphoreType.DMA((3, 2))],
        compiler_params=pltpu.CompilerParams(vmem_limit_bytes=8 * MIB),
        cost_estimate=pl.CostEstimate(flops=0, bytes_accessed=6 * size, transcendentals=0),
    )(*after, *in_hbm(w_gate, w_up, w_down))


def join_kernel(first_ref, second_ref, near_ref, out_ref):
    half = first_ref.shape[0]
    out_ref[:half] = first_ref[...]
    out_ref[half:] = second_ref[...]


def join(first, second, near):
    return pl.pallas_call(
        join_kernel,
        out_shape=pltpu.VMEM((2 * first.shape[0], first.shape[1]), first.dtype),
        in_specs=[VMEM, VMEM, pl.BlockSpec(memory_space=pl.ANY)],
        out_specs=VMEM,
        compiler_params=pltpu.CompilerParams(vmem_limit_bytes=4 * MIB),
    )(first, second, near)


def grads_kernel(pieces_in, *refs):
    parts = refs[:pieces_in]
    gate_ref, up_ref, down_ref, out_gate, out_up, out_down, rows_ref, buf, sems = refs[pieces_in:]
    start = 0
    for part in parts:
        rows_ref[pl.ds(start, part.shape[0])] = part[...]
        start += part.shape[0]
    rows = rows_ref[...]
    count, channels = rows.shape
    contract = (((1,), (1,)), ((), ()))
    gate_pre = lax.dot_general(rows, gate_ref[...], contract, preferred_element_type=jnp.float32)
    up_pre = lax.dot_general(rows, up_ref[...], contract, preferred_element_type=jnp.float32)
    is_x = lax.broadcasted_iota(jnp.int32, (count, 1), 0) % ROWS < CAP
    sig_gate = jax.nn.sigmoid(gate_pre)
    act_gate = gate_pre * sig_gate
    hidden = pltpu.roll(jnp.where(is_x, act_gate * up_pre, 0.0), CAP, 0)
    pieces = sems.shape[1]
    width = channels // pieces
    copies = []

    def outer(number, factor, out):
        turned = factor.T.astype(jnp.bfloat16)
        for part in range(pieces):
            cols = pl.ds(part * width, width)
            term = jnp.dot(turned, rows_ref[:, cols], preferred_element_type=jnp.float32)
            buf[number, :, cols] = term.astype(jnp.bfloat16)
            copy = pltpu.make_async_copy(buf.at[number, :, cols], out.at[:, cols], sems.at[number, part])
            copy.start()
            copies.append(copy)

    outer(0, hidden, out_down)
    back_grad = lax.dot_general(rows, down_ref[...], contract, preferred_element_type=jnp.float32)
    back_grad = pltpu.roll(back_grad, count - CAP, 0)
    outer(1, jnp.where(is_x, back_grad * act_gate, 0.0), out_up)
    d_gate = jnp.where(is_x, back_grad * up_pre * sig_gate * (1.0 + gate_pre * (1.0 - sig_gate)), 0.0)
    outer(2, d_gate, out_gate)
    for copy in copies:
        copy.wait()


def weight_grads(parts, w_gate, w_up, w_down):
    units, channels = w_gate.shape
    count = sum(part.shape[0] for part in parts)
    pieces = 4
    shape = jax.ShapeDtypeStruct((units, channels), jnp.bfloat16)
    return pl.pallas_call(
        functools.partial(grads_kernel, len(parts)),
        out_shape=(shape, shape, shape),
        in_specs=[VMEM] * (len(parts) + 3),
        out_specs=(HBM, HBM, HBM),
        scratch_shapes=[
            pltpu.VMEM((count, channels), jnp.bfloat16),
            pltpu.VMEM((3, units, channels), jnp.bfloat16),
            pltpu.SemaphoreType.DMA((3, pieces)),
        ],
        compiler_params=pltpu.CompilerParams(vmem_limit_bytes=24 * MIB),
    )(*parts, w_gate, w_up, w_down)


def swap(rows, axis, bits):
    count = lax.axis_size(axis)
    return lax.ppermute(rows, axis, [(place, place ^ bits) for place in range(count)])


def spread(rows):
    count = lax.axis_size("dp")
    if count > 4:
        return [lax.all_gather(rows, "dp", axis=0, tiled=True)]
    return [rows] + [swap(rows, "dp", bits) for bits in range(1, count)]


def local(tokens, expert_ids, gate_probs, out_grad, w_gate, w_up, w_down):
    experts = w_gate.shape[0] * lax.axis_size("expert")
    places = experts // 2
    own, other = pick_rows(experts, expert_ids.T, gate_probs.T, tokens, out_grad)
    other = swap(other, "expert", 1)
    blocks = []
    for place in range(places):
        cut = slice(place * ROWS, (place + 1) * ROWS)
        blocks.append(jnp.concatenate([own[cut], other[cut]]))
    arrived = [blocks[0]] + [swap(blocks[place], "expert", 2 * place) for place in range(1, places)]
    arrived[2:] = arrived[:1:-1]
    near = jnp.concatenate(arrived[: places // 2])
    middle = places // 4
    far = [jnp.concatenate(arrived[places // 2 :][:middle]), jnp.concatenate(arrived[places // 2 :][middle:])]
    far = join(far[0], far[1], near)
    parts = spread(near)
    gate, up, down = load_weights(parts + [far], w_gate[0], w_up[0], w_down[0])
    parts = parts + spread(far)
    grads = weight_grads(parts, gate, up, down)
    return tuple(grad[None] for grad in grads)


def solution(mesh):
    in_specs = (
        P(("expert", "dp"), None),
        P(("expert", "dp"), None),
        P(("expert", "dp"), None),
        P(("expert", "dp"), None),
        P("expert", "dp", None),
        P("expert", "dp", None),
        P("expert", "dp", None),
    )
    out_specs = (P("expert", "dp", None), P("expert", "dp", None), P("expert", "dp", None))
    return jax.shard_map(local, mesh=mesh, in_specs=in_specs, out_specs=out_specs, check_vma=False)
```

```python
import functools

import jax
import jax.numpy as jnp
from jax import lax
from jax.experimental import pallas as pl
from jax.experimental.pallas import tpu as pltpu
from jax.sharding import PartitionSpec as P

CAP = 2
ROWS = 2 * CAP
MIB = 1024 * 1024

VMEM = pl.BlockSpec(memory_space=pltpu.VMEM)
HBM = pl.BlockSpec(memory_space=pltpu.HBM)


def in_hbm(*arrays):
    return [pltpu.with_memory_space_constraint(array, pltpu.HBM) for array in arrays]


def pick_kernel(ids_hbm, probs_hbm, tokens_hbm, grad_hbm, own_ref, other_ref, ids_buf, probs_buf, buf, sems):
    copy_ids = pltpu.make_async_copy(ids_hbm, ids_buf, sems.at[0])
    copy_probs = pltpu.make_async_copy(probs_hbm, probs_buf, sems.at[1])
    copy_ids.start()
    copy_probs.start()
    pieces = (sems.shape[0] - 2) // 2
    top, count = ids_buf.shape
    width = buf.shape[1] // pieces
    copies = []
    for part in range(pieces):
        cols = pl.ds(part * width, width)
        for number, source in enumerate((tokens_hbm, grad_hbm)):
            copy = pltpu.make_async_copy(
                source.at[:, cols], buf.at[pl.ds(number * count, count), cols], sems.at[2 + 2 * part + number]
            )
            copy.start()
            copies.append(copy)
    half = own_ref.shape[0]
    total = 2 * half
    row = lax.broadcasted_iota(jnp.int32, (total, 1), 0)
    block = row // ROWS
    places = total // ROWS // 2
    relative = 2 * (block % places) + block // places
    expert = lax.axis_index("expert") ^ relative
    slot = (row % CAP).astype(jnp.float32)
    is_x = row % ROWS < CAP
    earlier = (
        lax.broadcasted_iota(jnp.int32, (count, count), 0)
        < lax.broadcasted_iota(jnp.int32, (count, count), 1)
    ).astype(jnp.bfloat16)
    copy_ids.wait()
    copy_probs.wait()
    named = jnp.zeros((total, count), jnp.float32)
    prob = jnp.zeros((total, count), jnp.float32)
    for k in range(top):
        hit = ids_buf[k : k + 1, :] == expert
        named = jnp.where(hit, 1.0, named)
        prob = jnp.where(hit, probs_buf[k : k + 1, :], prob)
    rank = jnp.dot(named.astype(jnp.bfloat16), earlier, preferred_element_type=jnp.float32)
    pick = jnp.where((named > 0.5) & (rank == slot), 1.0, 0.0)
    scale = jnp.where(is_x, 1.0, jnp.sum(pick * prob, axis=1, keepdims=True))
    picker = jnp.concatenate([jnp.where(is_x, pick, 0.0), jnp.where(is_x, 0.0, pick)], axis=1).astype(jnp.bfloat16)
    for part in range(pieces):
        cols = pl.ds(part * width, width)
        copies[2 * part].wait()
        copies[2 * part + 1].wait()
        rows = jnp.dot(picker, buf[:, cols], preferred_element_type=jnp.float32) * scale
        rows = rows.astype(jnp.bfloat16)
        own_ref[:, cols] = rows[:half]
        other_ref[:, cols] = rows[half:]


def pick_rows(experts, ids, probs, tokens, out_grad):
    top = ids.shape[0]
    count, channels = tokens.shape
    pieces = 4
    shape = pltpu.VMEM((experts * ROWS // 2, channels), jnp.bfloat16)
    return pl.pallas_call(
        pick_kernel,
        out_shape=(shape, shape),
        in_specs=[HBM] * 4,
        out_specs=(VMEM, VMEM),
        scratch_shapes=[
            pltpu.VMEM((top, count), jnp.int32),
            pltpu.VMEM((top, count), jnp.float32),
            pltpu.VMEM((2 * count, channels), jnp.bfloat16),
            pltpu.SemaphoreType.DMA((2 + 2 * pieces,)),
        ],
        compiler_params=pltpu.CompilerParams(vmem_limit_bytes=16 * MIB),
    )(*in_hbm(ids, probs, tokens, out_grad))


def load_kernel(*refs):
    gate_hbm, up_hbm, down_hbm, gate_ref, up_ref, down_ref, sems = refs[-7:]
    copies = []
    for number, (source, target) in enumerate(((gate_hbm, gate_ref), (up_hbm, up_ref), (down_hbm, down_ref))):
        half = source.shape[0] // 2
        for part in range(2):
            rows = pl.ds(part * half, half)
            copy = pltpu.make_async_copy(source.at[rows], target.at[rows], sems.at[number, part])
            copy.start()
            copies.append(copy)
    for copy in copies:
        copy.wait()


def load_weights(after, w_gate, w_up, w_down):
    shape = pltpu.VMEM(w_gate.shape, w_gate.dtype)
    size = w_gate.size * 2
    return pl.pallas_call(
        load_kernel,
        out_shape=(shape, shape, shape),
        in_specs=[pl.BlockSpec(memory_space=pl.ANY)] * len(after) + [HBM] * 3,
        out_specs=(VMEM, VMEM, VMEM),
        scratch_shapes=[pltpu.SemaphoreType.DMA((3, 2))],
        compiler_params=pltpu.CompilerParams(vmem_limit_bytes=8 * MIB),
        cost_estimate=pl.CostEstimate(flops=0, bytes_accessed=6 * size, transcendentals=0),
    )(*after, *in_hbm(w_gate, w_up, w_down))


def join_kernel(first_ref, second_ref, near_ref, out_ref):
    half = first_ref.shape[0]
    out_ref[:half] = first_ref[...]
    out_ref[half:] = second_ref[...]


def join(first, second, near):
    return pl.pallas_call(
        join_kernel,
        out_shape=pltpu.VMEM((2 * first.shape[0], first.shape[1]), first.dtype),
        in_specs=[VMEM, VMEM, pl.BlockSpec(memory_space=pl.ANY)],
        out_specs=VMEM,
        compiler_params=pltpu.CompilerParams(vmem_limit_bytes=4 * MIB),
        cost_estimate=pl.CostEstimate(flops=10**9, bytes_accessed=0, transcendentals=0),
    )(first, second, near)


def grads_kernel(pieces_in, *refs):
    parts = refs[:pieces_in]
    gate_ref, up_ref, down_ref, out_gate, out_up, out_down, rows_ref, buf, sems = refs[pieces_in:]
    start = 0
    for part in parts:
        rows_ref[pl.ds(start, part.shape[0])] = part[...]
        start += part.shape[0]
    rows = rows_ref[...]
    count, channels = rows.shape
    contract = (((1,), (1,)), ((), ()))
    gate_pre = lax.dot_general(gate_ref[...], rows, contract, preferred_element_type=jnp.float32)
    up_pre = lax.dot_general(up_ref[...], rows, contract, preferred_element_type=jnp.float32)
    back_grad = lax.dot_general(down_ref[...], rows, contract, preferred_element_type=jnp.float32)
    back_grad = pltpu.roll(back_grad, count - CAP, 1)
    is_x = lax.broadcasted_iota(jnp.int32, (1, count), 1) % ROWS < CAP
    sig_gate = jax.nn.sigmoid(gate_pre)
    act_gate = gate_pre * sig_gate
    pieces = sems.shape[1]
    width = channels // pieces
    copies = []

    def outer(number, factor, out):
        factor = factor.astype(jnp.bfloat16)
        for part in range(pieces):
            cols = pl.ds(part * width, width)
            term = jnp.dot(factor, rows_ref[:, cols], preferred_element_type=jnp.float32)
            buf[number, :, cols] = term.astype(jnp.bfloat16)
            copy = pltpu.make_async_copy(buf.at[number, :, cols], out.at[:, cols], sems.at[number, part])
            copy.start()
            copies.append(copy)

    outer(0, pltpu.roll(jnp.where(is_x, act_gate * up_pre, 0.0), CAP, 1), out_down)
    outer(1, jnp.where(is_x, back_grad * act_gate, 0.0), out_up)
    d_gate = jnp.where(is_x, back_grad * up_pre * sig_gate * (1.0 + gate_pre * (1.0 - sig_gate)), 0.0)
    outer(2, d_gate, out_gate)
    for copy in copies:
        copy.wait()


def weight_grads(parts, w_gate, w_up, w_down):
    units, channels = w_gate.shape
    count = sum(part.shape[0] for part in parts)
    pieces = 4
    shape = jax.ShapeDtypeStruct((units, channels), jnp.bfloat16)
    return pl.pallas_call(
        functools.partial(grads_kernel, len(parts)),
        out_shape=(shape, shape, shape),
        in_specs=[VMEM] * (len(parts) + 3),
        out_specs=(HBM, HBM, HBM),
        scratch_shapes=[
            pltpu.VMEM((count, channels), jnp.bfloat16),
            pltpu.VMEM((3, units, channels), jnp.bfloat16),
            pltpu.SemaphoreType.DMA((3, pieces)),
        ],
        compiler_params=pltpu.CompilerParams(vmem_limit_bytes=24 * MIB),
    )(*parts, w_gate, w_up, w_down)


def swap(rows, axis, bits):
    count = lax.axis_size(axis)
    return lax.ppermute(rows, axis, [(place, place ^ bits) for place in range(count)])


def spread(rows):
    count = lax.axis_size("dp")
    if count > 4:
        return [lax.all_gather(rows, "dp", axis=0, tiled=True)]
    return [rows] + [swap(rows, "dp", bits) for bits in range(1, count)]


def local(tokens, expert_ids, gate_probs, out_grad, w_gate, w_up, w_down):
    experts = w_gate.shape[0] * lax.axis_size("expert")
    places = experts // 2
    own, other = pick_rows(experts, expert_ids.T, gate_probs.T, tokens, out_grad)
    other = swap(other, "expert", 1)
    blocks = []
    for place in range(places):
        cut = slice(place * ROWS, (place + 1) * ROWS)
        blocks.append(jnp.concatenate([own[cut], other[cut]]))
    arrived = [blocks[0]] + [swap(blocks[place], "expert", 2 * place) for place in range(1, places)]
    near = jnp.concatenate(arrived[: places // 2])
    middle = places // 4
    far = [jnp.concatenate(arrived[places // 2 :][:middle]), jnp.concatenate(arrived[places // 2 :][middle:])]
    far = join(far[0], far[1], near)
    parts = spread(near)
    gate, up, down = load_weights(parts + [far], w_gate[0], w_up[0], w_down[0])
    parts = parts + spread(far)
    grads = weight_grads(parts, gate, up, down)
    return tuple(grad[None] for grad in grads)


def solution(mesh):
    in_specs = (
        P(("expert", "dp"), None),
        P(("expert", "dp"), None),
        P(("expert", "dp"), None),
        P(("expert", "dp"), None),
        P("expert", "dp", None),
        P("expert", "dp", None),
        P("expert", "dp", None),
    )
    out_specs = (P("expert", "dp", None), P("expert", "dp", None), P("expert", "dp", None))
    return jax.shard_map(local, mesh=mesh, in_specs=in_specs, out_specs=out_specs, check_vma=False)
```

```python
import functools

import jax
import jax.numpy as jnp
from jax import lax
from jax.experimental import pallas as pl
from jax.experimental.pallas import tpu as pltpu
from jax.sharding import PartitionSpec as P

CAP = 2
ROWS = 2 * CAP
MIB = 1024 * 1024

VMEM = pl.BlockSpec(memory_space=pltpu.VMEM)
HBM = pl.BlockSpec(memory_space=pltpu.HBM)


def in_hbm(*arrays):
    return [pltpu.with_memory_space_constraint(array, pltpu.HBM) for array in arrays]


def pick_kernel(ids_hbm, probs_hbm, tokens_hbm, grad_hbm, own_ref, other_ref, ids_buf, probs_buf, buf, sems):
    copy_ids = pltpu.make_async_copy(ids_hbm, ids_buf, sems.at[0])
    copy_probs = pltpu.make_async_copy(probs_hbm, probs_buf, sems.at[1])
    copy_ids.start()
    copy_probs.start()
    pieces = (sems.shape[0] - 2) // 2
    top, count = ids_buf.shape
    width = buf.shape[1] // pieces
    copies = []
    for part in range(pieces):
        cols = pl.ds(part * width, width)
        for number, source in enumerate((tokens_hbm, grad_hbm)):
            copy = pltpu.make_async_copy(
                source.at[:, cols], buf.at[pl.ds(number * count, count), cols], sems.at[2 + 2 * part + number]
            )
            copy.start()
            copies.append(copy)
    half = own_ref.shape[0]
    total = 2 * half
    row = lax.broadcasted_iota(jnp.int32, (total, 1), 0)
    block = row // ROWS
    places = total // ROWS // 2
    relative = 2 * (block % places) + block // places
    expert = lax.axis_index("expert") ^ relative
    slot = (row % CAP).astype(jnp.float32)
    is_x = row % ROWS < CAP
    earlier = (
        lax.broadcasted_iota(jnp.int32, (count, count), 0)
        < lax.broadcasted_iota(jnp.int32, (count, count), 1)
    ).astype(jnp.bfloat16)
    copy_ids.wait()
    copy_probs.wait()
    named = jnp.zeros((total, count), jnp.float32)
    prob = jnp.zeros((total, count), jnp.float32)
    for k in range(top):
        hit = ids_buf[k : k + 1, :] == expert
        named = jnp.where(hit, 1.0, named)
        prob = jnp.where(hit, probs_buf[k : k + 1, :], prob)
    rank = jnp.dot(named.astype(jnp.bfloat16), earlier, preferred_element_type=jnp.float32)
    pick = jnp.where((named > 0.5) & (rank == slot), 1.0, 0.0)
    scale = jnp.where(is_x, 1.0, jnp.sum(pick * prob, axis=1, keepdims=True))
    picker = jnp.concatenate([jnp.where(is_x, pick, 0.0), jnp.where(is_x, 0.0, pick)], axis=1).astype(jnp.bfloat16)
    for part in range(pieces):
        cols = pl.ds(part * width, width)
        copies[2 * part].wait()
        copies[2 * part + 1].wait()
        rows = jnp.dot(picker, buf[:, cols], preferred_element_type=jnp.float32) * scale
        rows = rows.astype(jnp.bfloat16)
        own_ref[:, cols] = rows[:half]
        other_ref[:, cols] = rows[half:]


def pick_rows(experts, ids, probs, tokens, out_grad):
    top = ids.shape[0]
    count, channels = tokens.shape
    pieces = 2
    shape = pltpu.VMEM((experts * ROWS // 2, channels), jnp.bfloat16)
    return pl.pallas_call(
        pick_kernel,
        out_shape=(shape, shape),
        in_specs=[HBM] * 4,
        out_specs=(VMEM, VMEM),
        scratch_shapes=[
            pltpu.VMEM((top, count), jnp.int32),
            pltpu.VMEM((top, count), jnp.float32),
            pltpu.VMEM((2 * count, channels), jnp.bfloat16),
            pltpu.SemaphoreType.DMA((2 + 2 * pieces,)),
        ],
        compiler_params=pltpu.CompilerParams(vmem_limit_bytes=16 * MIB),
    )(*in_hbm(ids, probs, tokens, out_grad))


def load_kernel(*refs):
    gate_hbm, up_hbm, down_hbm, gate_ref, up_ref, down_ref, sems = refs[-7:]
    copies = []
    for number, (source, target) in enumerate(((gate_hbm, gate_ref), (up_hbm, up_ref), (down_hbm, down_ref))):
        half = source.shape[0] // 2
        for part in range(2):
            rows = pl.ds(part * half, half)
            copy = pltpu.make_async_copy(source.at[rows], target.at[rows], sems.at[number, part])
            copy.start()
            copies.append(copy)
    for copy in copies:
        copy.wait()


def load_weights(after, w_gate, w_up, w_down):
    shape = pltpu.VMEM(w_gate.shape, w_gate.dtype)
    size = w_gate.size * 2
    return pl.pallas_call(
        load_kernel,
        out_shape=(shape, shape, shape),
        in_specs=[pl.BlockSpec(memory_space=pl.ANY)] * len(after) + [HBM] * 3,
        out_specs=(VMEM, VMEM, VMEM),
        scratch_shapes=[pltpu.SemaphoreType.DMA((3, 2))],
        compiler_params=pltpu.CompilerParams(vmem_limit_bytes=8 * MIB),
        cost_estimate=pl.CostEstimate(flops=0, bytes_accessed=6 * size, transcendentals=0),
    )(*after, *in_hbm(w_gate, w_up, w_down))


def deal_kernel(own_ref, other_ref, *blocks):
    for place, block in enumerate(blocks):
        cut = slice(place * ROWS, (place + 1) * ROWS)
        block[:ROWS] = own_ref[cut]
        block[ROWS:] = other_ref[cut]


def deal(own, other):
    places = own.shape[0] // ROWS
    return pl.pallas_call(
        deal_kernel,
        out_shape=[pltpu.VMEM((2 * ROWS, own.shape[1]), own.dtype)] * places,
        in_specs=[VMEM, VMEM],
        out_specs=[VMEM] * places,
        compiler_params=pltpu.CompilerParams(vmem_limit_bytes=8 * MIB),
    )(own, other)


def join_kernel(first_ref, *refs):
    *_, out_ref = refs
    pieces = (first_ref,) + refs[: out_ref.shape[0] // first_ref.shape[0] - 1]
    size = first_ref.shape[0]
    for place, piece in enumerate(pieces):
        out_ref[place * size : (place + 1) * size] = piece[...]


def join(pieces, after=(), flops=0):
    size, channels = pieces[0].shape
    return pl.pallas_call(
        join_kernel,
        out_shape=pltpu.VMEM((len(pieces) * size, channels), pieces[0].dtype),
        in_specs=[VMEM] * len(pieces) + [pl.BlockSpec(memory_space=pl.ANY)] * len(after),
        out_specs=VMEM,
        compiler_params=pltpu.CompilerParams(vmem_limit_bytes=8 * MIB),
        cost_estimate=pl.CostEstimate(flops=flops, bytes_accessed=0, transcendentals=0),
    )(*pieces, *after)


def grads_kernel(pieces_in, *refs):
    parts = refs[:pieces_in]
    gate_ref, up_ref, down_ref, out_gate, out_up, out_down, rows_ref, buf, sems = refs[pieces_in:]
    rows = jnp.concatenate([part[...] for part in parts], axis=0)
    rows_ref[...] = rows
    count, channels = rows.shape
    contract = (((1,), (1,)), ((), ()))
    gate_pre = lax.dot_general(gate_ref[...], rows, contract, preferred_element_type=jnp.float32)
    up_pre = lax.dot_general(up_ref[...], rows, contract, preferred_element_type=jnp.float32)
    back_grad = lax.dot_general(down_ref[...], rows, contract, preferred_element_type=jnp.float32)
    back_grad = pltpu.roll(back_grad, count - CAP, 1)
    is_x = lax.broadcasted_iota(jnp.int32, (1, count), 1) % ROWS < CAP
    sig_gate = jax.nn.sigmoid(gate_pre)
    act_gate = gate_pre * sig_gate
    pieces = sems.shape[1]
    width = channels // pieces
    copies = []

    def outer(number, factor, out):
        factor = factor.astype(jnp.bfloat16)
        for part in range(pieces):
            cols = pl.ds(part * width, width)
            term = jnp.dot(factor, rows_ref[:, cols], preferred_element_type=jnp.float32)
            buf[number, :, cols] = term.astype(jnp.bfloat16)
            copy = pltpu.make_async_copy(buf.at[number, :, cols], out.at[:, cols], sems.at[number, part])
            copy.start()
            copies.append(copy)

    outer(0, pltpu.roll(jnp.where(is_x, act_gate * up_pre, 0.0), CAP, 1), out_down)
    outer(1, jnp.where(is_x, back_grad * act_gate, 0.0), out_up)
    d_gate = jnp.where(is_x, back_grad * up_pre * sig_gate * (1.0 + gate_pre * (1.0 - sig_gate)), 0.0)
    outer(2, d_gate, out_gate)
    for copy in copies:
        copy.wait()


def weight_grads(parts, w_gate, w_up, w_down):
    units, channels = w_gate.shape
    count = sum(part.shape[0] for part in parts)
    pieces = 4
    shape = jax.ShapeDtypeStruct((units, channels), jnp.bfloat16)
    return pl.pallas_call(
        functools.partial(grads_kernel, len(parts)),
        out_shape=(shape, shape, shape),
        in_specs=[VMEM] * (len(parts) + 3),
        out_specs=(HBM, HBM, HBM),
        scratch_shapes=[
            pltpu.VMEM((count, channels), jnp.bfloat16),
            pltpu.VMEM((3, units, channels), jnp.bfloat16),
            pltpu.SemaphoreType.DMA((3, pieces)),
        ],
        compiler_params=pltpu.CompilerParams(vmem_limit_bytes=24 * MIB),
    )(*parts, w_gate, w_up, w_down)


def swap(rows, axis, bits):
    count = lax.axis_size(axis)
    return lax.ppermute(rows, axis, [(place, place ^ bits) for place in range(count)])


def spread(rows):
    count = lax.axis_size("dp")
    if count > 4:
        return [lax.all_gather(rows, "dp", axis=0, tiled=True)]
    return [rows] + [swap(rows, "dp", bits) for bits in range(1, count)]


def local(tokens, expert_ids, gate_probs, out_grad, w_gate, w_up, w_down):
    experts = w_gate.shape[0] * lax.axis_size("expert")
    near_places = experts // 4
    own, other = pick_rows(experts, expert_ids.T, gate_probs.T, tokens, out_grad)
    blocks = deal(own, swap(other, "expert", 1))
    arrived = [swap(block, "expert", 2 * place) if place else block for place, block in enumerate(blocks)]
    near = join(arrived[:near_places], flops=0)
    far = join(arrived[near_places:], after=(near,), flops=10**9)
    parts = spread(near)
    gate, up, down = load_weights(parts + [far], w_gate[0], w_up[0], w_down[0])
    parts = parts + spread(far)
    grads = weight_grads(parts, gate, up, down)
    return tuple(grad[None] for grad in grads)


def solution(mesh):
    in_specs = (
        P(("expert", "dp"), None),
        P(("expert", "dp"), None),
        P(("expert", "dp"), None),
        P(("expert", "dp"), None),
        P("expert", "dp", None),
        P("expert", "dp", None),
        P("expert", "dp", None),
    )
    out_specs = (P("expert", "dp", None), P("expert", "dp", None), P("expert", "dp", None))
    return jax.shard_map(local, mesh=mesh, in_specs=in_specs, out_specs=out_specs, check_vma=False)
```

```python
import functools

import jax
import jax.numpy as jnp
from jax import lax
from jax.experimental import pallas as pl
from jax.experimental.pallas import tpu as pltpu
from jax.sharding import PartitionSpec as P

CAP = 2
ROWS = 2 * CAP
MIB = 1024 * 1024

VMEM = pl.BlockSpec(memory_space=pltpu.VMEM)
HBM = pl.BlockSpec(memory_space=pltpu.HBM)


def in_hbm(*arrays):
    return [pltpu.with_memory_space_constraint(array, pltpu.HBM) for array in arrays]


def pick_kernel(ids_hbm, probs_hbm, tokens_hbm, grad_hbm, own_ref, other_ref, ids_buf, probs_buf, buf, sems):
    copy_ids = pltpu.make_async_copy(ids_hbm, ids_buf, sems.at[0])
    copy_probs = pltpu.make_async_copy(probs_hbm, probs_buf, sems.at[1])
    copy_ids.start()
    copy_probs.start()
    pieces = (sems.shape[0] - 2) // 2
    top, count = ids_buf.shape
    width = buf.shape[1] // pieces
    copies = []
    for part in range(pieces):
        cols = pl.ds(part * width, width)
        for number, source in enumerate((tokens_hbm, grad_hbm)):
            copy = pltpu.make_async_copy(
                source.at[:, cols], buf.at[pl.ds(number * count, count), cols], sems.at[2 + 2 * part + number]
            )
            copy.start()
            copies.append(copy)
    half = own_ref.shape[0]
    total = 2 * half
    row = lax.broadcasted_iota(jnp.int32, (total, 1), 0)
    block = row // ROWS
    places = total // ROWS // 2
    place, other = block % places, block // places
    me = lax.axis_index("expert")
    along = jnp.where(2 * place >= places, place ^ ((me ^ other ^ 1) & 1), place)
    expert = me ^ (2 * along + other)
    slot = (row % CAP).astype(jnp.float32)
    is_x = row % ROWS < CAP
    earlier = (
        lax.broadcasted_iota(jnp.int32, (count, count), 0)
        < lax.broadcasted_iota(jnp.int32, (count, count), 1)
    ).astype(jnp.bfloat16)
    copy_ids.wait()
    copy_probs.wait()
    named = jnp.zeros((total, count), jnp.float32)
    prob = jnp.zeros((total, count), jnp.float32)
    for k in range(top):
        hit = ids_buf[k : k + 1, :] == expert
        named = jnp.where(hit, 1.0, named)
        prob = jnp.where(hit, probs_buf[k : k + 1, :], prob)
    rank = jnp.dot(named.astype(jnp.bfloat16), earlier, preferred_element_type=jnp.float32)
    pick = jnp.where((named > 0.5) & (rank == slot), 1.0, 0.0)
    scale = jnp.where(is_x, 1.0, jnp.sum(pick * prob, axis=1, keepdims=True))
    picker = jnp.concatenate([jnp.where(is_x, pick, 0.0), jnp.where(is_x, 0.0, pick)], axis=1).astype(jnp.bfloat16)
    for part in range(pieces):
        cols = pl.ds(part * width, width)
        copies[2 * part].wait()
        copies[2 * part + 1].wait()
        rows = jnp.dot(picker, buf[:, cols], preferred_element_type=jnp.float32) * scale
        rows = rows.astype(jnp.bfloat16)
        own_ref[:, cols] = rows[:half]
        other_ref[:, cols] = rows[half:]


def pick_rows(experts, ids, probs, tokens, out_grad):
    top = ids.shape[0]
    count, channels = tokens.shape
    pieces = 2
    shape = pltpu.VMEM((experts * ROWS // 2, channels), jnp.bfloat16)
    return pl.pallas_call(
        pick_kernel,
        out_shape=(shape, shape),
        in_specs=[HBM] * 4,
        out_specs=(VMEM, VMEM),
        scratch_shapes=[
            pltpu.VMEM((top, count), jnp.int32),
            pltpu.VMEM((top, count), jnp.float32),
            pltpu.VMEM((2 * count, channels), jnp.bfloat16),
            pltpu.SemaphoreType.DMA((2 + 2 * pieces,)),
        ],
        compiler_params=pltpu.CompilerParams(vmem_limit_bytes=16 * MIB),
    )(*in_hbm(ids, probs, tokens, out_grad))


def load_kernel(*refs):
    gate_hbm, up_hbm, down_hbm, gate_ref, up_ref, down_ref, sems = refs[-7:]
    copies = []
    for number, (source, target) in enumerate(((gate_hbm, gate_ref), (up_hbm, up_ref), (down_hbm, down_ref))):
        half = source.shape[0] // 2
        for part in range(2):
            rows = pl.ds(part * half, half)
            copy = pltpu.make_async_copy(source.at[rows], target.at[rows], sems.at[number, part])
            copy.start()
            copies.append(copy)
    for copy in copies:
        copy.wait()


def load_weights(after, w_gate, w_up, w_down):
    shape = pltpu.VMEM(w_gate.shape, w_gate.dtype)
    size = w_gate.size * 2
    return pl.pallas_call(
        load_kernel,
        out_shape=(shape, shape, shape),
        in_specs=[pl.BlockSpec(memory_space=pl.ANY)] * len(after) + [HBM] * 3,
        out_specs=(VMEM, VMEM, VMEM),
        scratch_shapes=[pltpu.SemaphoreType.DMA((3, 2))],
        compiler_params=pltpu.CompilerParams(vmem_limit_bytes=8 * MIB),
        cost_estimate=pl.CostEstimate(flops=0, bytes_accessed=6 * size, transcendentals=0),
    )(*after, *in_hbm(w_gate, w_up, w_down))


def deal_kernel(own_ref, other_ref, *blocks):
    for place, block in enumerate(blocks):
        cut = slice(place * ROWS, (place + 1) * ROWS)
        block[:ROWS] = own_ref[cut]
        block[ROWS:] = other_ref[cut]


def deal(own, other):
    places = own.shape[0] // ROWS
    return pl.pallas_call(
        deal_kernel,
        out_shape=[pltpu.VMEM((2 * ROWS, own.shape[1]), own.dtype)] * places,
        in_specs=[VMEM, VMEM],
        out_specs=[VMEM] * places,
        compiler_params=pltpu.CompilerParams(vmem_limit_bytes=8 * MIB),
    )(own, other)


def join_kernel(first_ref, *refs):
    *_, out_ref = refs
    pieces = (first_ref,) + refs[: out_ref.shape[0] // first_ref.shape[0] - 1]
    size = first_ref.shape[0]
    for place, piece in enumerate(pieces):
        out_ref[place * size : (place + 1) * size] = piece[...]


def join(pieces, after=(), flops=0):
    size, channels = pieces[0].shape
    return pl.pallas_call(
        join_kernel,
        out_shape=pltpu.VMEM((len(pieces) * size, channels), pieces[0].dtype),
        in_specs=[VMEM] * len(pieces) + [pl.BlockSpec(memory_space=pl.ANY)] * len(after),
        out_specs=VMEM,
        compiler_params=pltpu.CompilerParams(vmem_limit_bytes=8 * MIB),
        cost_estimate=pl.CostEstimate(flops=flops, bytes_accessed=0, transcendentals=0),
    )(*pieces, *after)


def grads_kernel(pieces_in, *refs):
    parts = refs[:pieces_in]
    gate_ref, up_ref, down_ref, out_gate, out_up, out_down, rows_ref, buf, sems = refs[pieces_in:]
    rows = jnp.concatenate([part[...] for part in parts], axis=0)
    rows_ref[...] = rows
    count, channels = rows.shape
    contract = (((1,), (1,)), ((), ()))
    gate_pre = lax.dot_general(gate_ref[...], rows, contract, preferred_element_type=jnp.float32)
    up_pre = lax.dot_general(up_ref[...], rows, contract, preferred_element_type=jnp.float32)
    back_grad = lax.dot_general(down_ref[...], rows, contract, preferred_element_type=jnp.float32)
    back_grad = pltpu.roll(back_grad, count - CAP, 1)
    is_x = lax.broadcasted_iota(jnp.int32, (1, count), 1) % ROWS < CAP
    sig_gate = jax.nn.sigmoid(gate_pre)
    act_gate = gate_pre * sig_gate
    pieces = sems.shape[1]
    width = channels // pieces
    copies = []

    def outer(number, factor, out):
        factor = factor.astype(jnp.bfloat16)
        for part in range(pieces):
            cols = pl.ds(part * width, width)
            term = jnp.dot(factor, rows_ref[:, cols], preferred_element_type=jnp.float32)
            buf[number, :, cols] = term.astype(jnp.bfloat16)
            copy = pltpu.make_async_copy(buf.at[number, :, cols], out.at[:, cols], sems.at[number, part])
            copy.start()
            copies.append(copy)

    outer(0, pltpu.roll(jnp.where(is_x, act_gate * up_pre, 0.0), CAP, 1), out_down)
    outer(1, jnp.where(is_x, back_grad * act_gate, 0.0), out_up)
    d_gate = jnp.where(is_x, back_grad * up_pre * sig_gate * (1.0 + gate_pre * (1.0 - sig_gate)), 0.0)
    outer(2, d_gate, out_gate)
    for copy in copies:
        copy.wait()


def weight_grads(parts, w_gate, w_up, w_down):
    units, channels = w_gate.shape
    count = sum(part.shape[0] for part in parts)
    pieces = 4
    shape = jax.ShapeDtypeStruct((units, channels), jnp.bfloat16)
    return pl.pallas_call(
        functools.partial(grads_kernel, len(parts)),
        out_shape=(shape, shape, shape),
        in_specs=[VMEM] * (len(parts) + 3),
        out_specs=(HBM, HBM, HBM),
        scratch_shapes=[
            pltpu.VMEM((count, channels), jnp.bfloat16),
            pltpu.VMEM((3, units, channels), jnp.bfloat16),
            pltpu.SemaphoreType.DMA((3, pieces)),
        ],
        compiler_params=pltpu.CompilerParams(vmem_limit_bytes=24 * MIB),
    )(*parts, w_gate, w_up, w_down)


def swap(rows, axis, bits):
    count = lax.axis_size(axis)
    return lax.ppermute(rows, axis, [(place, place ^ bits) for place in range(count)])


def swap_by_core(rows, bits):
    experts, count = lax.axis_size("expert"), lax.axis_size("dp")
    pairs = []
    for expert in range(experts):
        for place in range(count):
            pairs.append((expert * count + place, expert * count + (place ^ bits[expert % 2])))
    return lax.ppermute(rows, ("expert", "dp"), pairs)


def spread(rows):
    count = lax.axis_size("dp")
    if count > 4:
        return [lax.all_gather(rows, "dp", axis=0, tiled=True)]
    if count < 4:
        return [rows] + [swap(rows, "dp", bits) for bits in range(1, count)]
    return [rows, swap_by_core(rows, (1, 2)), swap_by_core(rows, (2, 1)), swap(rows, "dp", 3)]


def local(tokens, expert_ids, gate_probs, out_grad, w_gate, w_up, w_down):
    experts = w_gate.shape[0] * lax.axis_size("expert")
    near_places = experts // 4
    own, other = pick_rows(experts, expert_ids.T, gate_probs.T, tokens, out_grad)
    blocks = deal(own, swap(other, "expert", 1))
    arrived = []
    for place, block in enumerate(blocks):
        along = [place ^ 1, place] if place >= near_places else [place, place]
        pairs = [(expert, expert ^ (2 * along[expert % 2])) for expert in range(experts)]
        arrived.append(lax.ppermute(block, "expert", pairs) if place else block)
    near = join(arrived[:near_places], flops=0)
    far = join(arrived[near_places:], after=(near,), flops=10**9)
    parts = spread(near)
    gate, up, down = load_weights(parts + [far], w_gate[0], w_up[0], w_down[0])
    parts = parts + spread(far)
    grads = weight_grads(parts, gate, up, down)
    return tuple(grad[None] for grad in grads)


def solution(mesh):
    in_specs = (
        P(("expert", "dp"), None),
        P(("expert", "dp"), None),
        P(("expert", "dp"), None),
        P(("expert", "dp"), None),
        P("expert", "dp", None),
        P("expert", "dp", None),
        P("expert", "dp", None),
    )
    out_specs = (P("expert", "dp", None), P("expert", "dp", None), P("expert", "dp", None))
    return jax.shard_map(local, mesh=mesh, in_specs=in_specs, out_specs=out_specs, check_vma=False)
```

```python
import functools

import jax
import jax.numpy as jnp
from jax import lax
from jax.experimental import pallas as pl
from jax.experimental.pallas import tpu as pltpu
from jax.sharding import PartitionSpec as P

CAP = 2
ROWS = 2 * CAP
MIB = 1024 * 1024

VMEM = pl.BlockSpec(memory_space=pltpu.VMEM)
HBM = pl.BlockSpec(memory_space=pltpu.HBM)


def in_hbm(*arrays):
    return [pltpu.with_memory_space_constraint(array, pltpu.HBM) for array in arrays]


def pick_kernel(ids_hbm, probs_hbm, tokens_hbm, grad_hbm, own_ref, other_ref, ids_buf, probs_buf, buf, sems):
    copy_ids = pltpu.make_async_copy(ids_hbm, ids_buf, sems.at[0])
    copy_probs = pltpu.make_async_copy(probs_hbm, probs_buf, sems.at[1])
    copy_ids.start()
    copy_probs.start()
    pieces = (sems.shape[0] - 2) // 2
    top, count = ids_buf.shape
    width = buf.shape[1] // pieces
    copies = []
    for part in range(pieces):
        cols = pl.ds(part * width, width)
        for number, source in enumerate((tokens_hbm, grad_hbm)):
            copy = pltpu.make_async_copy(
                source.at[:, cols], buf.at[pl.ds(number * count, count), cols], sems.at[2 + 2 * part + number]
            )
            copy.start()
            copies.append(copy)
    half = own_ref.shape[0]
    total = 2 * half
    row = lax.broadcasted_iota(jnp.int32, (total, 1), 0)
    block = row // ROWS
    places = total // ROWS // 2
    place, other = block % places, block // places
    me = lax.axis_index("expert")
    along = jnp.where(2 * place >= places, place ^ ((me ^ other ^ 1) & 1), place)
    expert = me ^ (2 * along + other)
    slot = (row % CAP).astype(jnp.float32)
    is_x = row % ROWS < CAP
    earlier = (
        lax.broadcasted_iota(jnp.int32, (count, count), 0)
        < lax.broadcasted_iota(jnp.int32, (count, count), 1)
    ).astype(jnp.bfloat16)
    copy_ids.wait()
    copy_probs.wait()
    named = jnp.zeros((total, count), jnp.float32)
    prob = jnp.zeros((total, count), jnp.float32)
    for k in range(top):
        hit = ids_buf[k : k + 1, :] == expert
        named = jnp.where(hit, 1.0, named)
        prob = jnp.where(hit, probs_buf[k : k + 1, :], prob)
    rank = jnp.dot(named.astype(jnp.bfloat16), earlier, preferred_element_type=jnp.float32)
    pick = jnp.where((named > 0.5) & (rank == slot), 1.0, 0.0)
    scale = jnp.where(is_x, 1.0, jnp.sum(pick * prob, axis=1, keepdims=True))
    picker = jnp.concatenate([jnp.where(is_x, pick, 0.0), jnp.where(is_x, 0.0, pick)], axis=1).astype(jnp.bfloat16)
    for part in range(pieces):
        cols = pl.ds(part * width, width)
        copies[2 * part].wait()
        copies[2 * part + 1].wait()
        rows = jnp.dot(picker, buf[:, cols], preferred_element_type=jnp.float32) * scale
        rows = rows.astype(jnp.bfloat16)
        own_ref[:, cols] = rows[:half]
        other_ref[:, cols] = rows[half:]


def pick_rows(experts, ids, probs, tokens, out_grad):
    top = ids.shape[0]
    count, channels = tokens.shape
    pieces = 2
    shape = pltpu.VMEM((experts * ROWS // 2, channels), jnp.bfloat16)
    return pl.pallas_call(
        pick_kernel,
        out_shape=(shape, shape),
        in_specs=[HBM] * 4,
        out_specs=(VMEM, VMEM),
        scratch_shapes=[
            pltpu.VMEM((top, count), jnp.int32),
            pltpu.VMEM((top, count), jnp.float32),
            pltpu.VMEM((2 * count, channels), jnp.bfloat16),
            pltpu.SemaphoreType.DMA((2 + 2 * pieces,)),
        ],
        compiler_params=pltpu.CompilerParams(vmem_limit_bytes=16 * MIB),
    )(*in_hbm(ids, probs, tokens, out_grad))


def load_kernel(*refs):
    gate_hbm, up_hbm, down_hbm, gate_ref, up_ref, down_ref, sems = refs[-7:]
    copies = []
    for number, (source, target) in enumerate(((gate_hbm, gate_ref), (up_hbm, up_ref), (down_hbm, down_ref))):
        half = source.shape[0] // 2
        for part in range(2):
            rows = pl.ds(part * half, half)
            copy = pltpu.make_async_copy(source.at[rows], target.at[rows], sems.at[number, part])
            copy.start()
            copies.append(copy)
    for copy in copies:
        copy.wait()


def load_weights(after, w_gate, w_up, w_down):
    shape = pltpu.VMEM(w_gate.shape, w_gate.dtype)
    size = w_gate.size * 2
    return pl.pallas_call(
        load_kernel,
        out_shape=(shape, shape, shape),
        in_specs=[pl.BlockSpec(memory_space=pl.ANY)] * len(after) + [HBM] * 3,
        out_specs=(VMEM, VMEM, VMEM),
        scratch_shapes=[pltpu.SemaphoreType.DMA((3, 2))],
        compiler_params=pltpu.CompilerParams(vmem_limit_bytes=8 * MIB),
        cost_estimate=pl.CostEstimate(flops=0, bytes_accessed=6 * size, transcendentals=0),
    )(*after, *in_hbm(w_gate, w_up, w_down))


def deal_kernel(own_ref, other_ref, *blocks):
    for place, block in enumerate(blocks):
        cut = slice(place * ROWS, (place + 1) * ROWS)
        block[:ROWS] = own_ref[cut]
        block[ROWS:] = other_ref[cut]


def deal(own, other):
    places = own.shape[0] // ROWS
    return pl.pallas_call(
        deal_kernel,
        out_shape=[pltpu.VMEM((2 * ROWS, own.shape[1]), own.dtype)] * places,
        in_specs=[VMEM, VMEM],
        out_specs=[VMEM] * places,
        compiler_params=pltpu.CompilerParams(vmem_limit_bytes=8 * MIB),
    )(own, other)


def join_kernel(first_ref, *refs):
    *_, out_ref = refs
    pieces = (first_ref,) + refs[: out_ref.shape[0] // first_ref.shape[0] - 1]
    size = first_ref.shape[0]
    for place, piece in enumerate(pieces):
        out_ref[place * size : (place + 1) * size] = piece[...]


def join(pieces, after=(), flops=0):
    size, channels = pieces[0].shape
    return pl.pallas_call(
        join_kernel,
        out_shape=pltpu.VMEM((len(pieces) * size, channels), pieces[0].dtype),
        in_specs=[VMEM] * len(pieces) + [pl.BlockSpec(memory_space=pl.ANY)] * len(after),
        out_specs=VMEM,
        compiler_params=pltpu.CompilerParams(vmem_limit_bytes=8 * MIB),
        cost_estimate=pl.CostEstimate(flops=flops, bytes_accessed=0, transcendentals=0),
    )(*pieces, *after)


def grads_kernel(pieces_in, *refs):
    parts = refs[:pieces_in]
    gate_ref, up_ref, down_ref, out_gate, out_up, out_down, rows_ref, buf, sems = refs[pieces_in:]
    rows = jnp.concatenate([part[...] for part in parts], axis=0)
    rows_ref[...] = rows
    count, channels = rows.shape
    contract = (((1,), (1,)), ((), ()))
    gate_pre = lax.dot_general(gate_ref[...], rows, contract, preferred_element_type=jnp.float32)
    up_pre = lax.dot_general(up_ref[...], rows, contract, preferred_element_type=jnp.float32)
    back_grad = lax.dot_general(down_ref[...], rows, contract, preferred_element_type=jnp.float32)
    back_grad = pltpu.roll(back_grad, count - CAP, 1)
    is_x = lax.broadcasted_iota(jnp.int32, (1, count), 1) % ROWS < CAP
    sig_gate = jax.nn.sigmoid(gate_pre)
    act_gate = gate_pre * sig_gate
    pieces = sems.shape[1]
    width = channels // pieces
    copies = []

    def outer(number, factor, out):
        factor = factor.astype(jnp.bfloat16)
        for part in range(pieces):
            cols = pl.ds(part * width, width)
            term = jnp.dot(factor, rows_ref[:, cols], preferred_element_type=jnp.float32)
            buf[number, :, cols] = term.astype(jnp.bfloat16)
            copy = pltpu.make_async_copy(buf.at[number, :, cols], out.at[:, cols], sems.at[number, part])
            copy.start()
            copies.append(copy)

    outer(0, pltpu.roll(jnp.where(is_x, act_gate * up_pre, 0.0), CAP, 1), out_down)
    outer(1, jnp.where(is_x, back_grad * act_gate, 0.0), out_up)
    d_gate = jnp.where(is_x, back_grad * up_pre * sig_gate * (1.0 + gate_pre * (1.0 - sig_gate)), 0.0)
    outer(2, d_gate, out_gate)
    for copy in copies:
        copy.wait()


def weight_grads(parts, w_gate, w_up, w_down):
    units, channels = w_gate.shape
    count = sum(part.shape[0] for part in parts)
    pieces = 4
    shape = jax.ShapeDtypeStruct((units, channels), jnp.bfloat16)
    return pl.pallas_call(
        functools.partial(grads_kernel, len(parts)),
        out_shape=(shape, shape, shape),
        in_specs=[VMEM] * (len(parts) + 3),
        out_specs=(HBM, HBM, HBM),
        scratch_shapes=[
            pltpu.VMEM((count, channels), jnp.bfloat16),
            pltpu.VMEM((3, units, channels), jnp.bfloat16),
            pltpu.SemaphoreType.DMA((3, pieces)),
        ],
        compiler_params=pltpu.CompilerParams(vmem_limit_bytes=24 * MIB),
    )(*parts, w_gate, w_up, w_down)


def swap(rows, axis, bits):
    count = lax.axis_size(axis)
    return lax.ppermute(rows, axis, [(place, place ^ bits) for place in range(count)])


def spread(rows):
    count = lax.axis_size("dp")
    if count > 4:
        return [lax.all_gather(rows, "dp", axis=0, tiled=True)]
    return [rows] + [swap(rows, "dp", bits) for bits in range(1, count)]


def local(tokens, expert_ids, gate_probs, out_grad, w_gate, w_up, w_down):
    experts = w_gate.shape[0] * lax.axis_size("expert")
    near_places = experts // 4
    own, other = pick_rows(experts, expert_ids.T, gate_probs.T, tokens, out_grad)
    blocks = deal(own, swap(other, "expert", 1))
    arrived = []
    for place, block in enumerate(blocks):
        along = [place ^ 1, place] if place >= near_places else [place, place]
        pairs = [(expert, expert ^ (2 * along[expert % 2])) for expert in range(experts)]
        arrived.append(lax.ppermute(block, "expert", pairs) if place else block)
    near = join(arrived[:near_places], flops=0)
    far = join(arrived[near_places:], after=(near,), flops=10**9)
    parts = spread(near)
    gate, up, down = load_weights(parts + [far], w_gate[0], w_up[0], w_down[0])
    parts = parts + spread(far)
    grads = weight_grads(parts, gate, up, down)
    return tuple(grad[None] for grad in grads)


def solution(mesh):
    in_specs = (
        P(("expert", "dp"), None),
        P(("expert", "dp"), None),
        P(("expert", "dp"), None),
        P(("expert", "dp"), None),
        P("expert", "dp", None),
        P("expert", "dp", None),
        P("expert", "dp", None),
    )
    out_specs = (P("expert", "dp", None), P("expert", "dp", None), P("expert", "dp", None))
    return jax.shard_map(local, mesh=mesh, in_specs=in_specs, out_specs=out_specs, check_vma=False)
```
